32 devices in a mesh: groups: 2 (over y), row: 8 (over z, x), col: 2 (over core).
Axes of the slice: x: 2, y: 2, z: 4, core: 2. Of those that a mesh axis runs over, the one named last changes fastest.
Arguments:
- inputs: bfloat16 [1024, 8192], P(('groups', 'row'), 'col'), parts along dimension 0, may hold values from -6 to 6
- gate_saved: bfloat16 [1024, 16384], P(('groups', 'col'), 'row'), parts along dimension 0, may hold values from -8 to 8
- up_saved: bfloat16 [1024, 16384], P(('groups', 'col'), 'row'), parts along dimension 0, may hold values from -6 to 6
- cotangent: bfloat16 [1024, 8192], P(('groups', 'row'), 'col'), parts along dimension 0, may hold values from -2 to 2
- gate_weight: bfloat16 [8192, 16384], P('col', 'row'), may hold values from -0.0625 to 0.0625
- up_weight: bfloat16 [8192, 16384], P('col', 'row'), may hold values from -0.0625 to 0.0625
- down_weight: bfloat16 [16384, 8192], P('row', 'col'), may hold values from -0.046875 to 0.046875
Outputs:
- grad_inputs: bfloat16 [1024, 8192], P(('groups', 'row'), 'col'), parts along dimension 0
- grad_gate: bfloat16 [16384, 16384], P(('groups', 'col'), 'row'), parts along dimension 0
- grad_up: bfloat16 [16384, 16384], P(('groups', 'col'), 'row'), parts along dimension 0
- grad_down: bfloat16 [32768, 8192], P(('groups', 'row'), 'col'), parts along dimension 0
The draws below stay inside these ranges and needn't reach their ends.
There are 2 independent parts, one for each index of `groups`. The reference program is written for one: setup_inputs(seed, part) draws one part's arguments, and reference() takes and returns one part's arrays. A program takes and returns all parts, laid end to end along the dimension named above; an argument that names none is the same for every part. Nothing has to cross between parts.
All inputs are finite; a program needn't handle non-finite values.
Results may differ from the reference program's by a relative error of at most 0.0051.
Values may be sent and summed in bfloat16 or wider, within the bound.
A program may use at most 256 MiB of HBM per device.

```python
import jax
import jax.numpy as jnp
from jax import lax

D = 8192
FF = 16384
TOKENS = 512


def spiked(values, key, source, target, shards_of, factor):
    def block_of(axis_at):
        return (jnp.arange(values.shape[axis_at]) // (values.shape[axis_at] // shards_of)).reshape((-1,) + (1,) * (values.ndim - 1 - axis_at))

    near = jax.random.permutation(key, shards_of)[block_of(target)]
    other_side = (block_of(target) + shards_of // 2) % shards_of
    return jnp.where((block_of(source) == near) | (block_of(source) == other_side), factor * values, values)


def steps_of(own_key, extent, split, low, top_value):
    factor_of = 1.0
    for dim, shards_of in split:
        draws = jax.random.uniform(jax.random.fold_in(jax.random.fold_in(own_key, 6), dim), (shards_of,), jnp.float32, low / len(split), top_value / len(split))
        factor_of = factor_of * jnp.repeat(jnp.exp(draws), extent[dim] // shards_of).reshape((-1,) + (1,) * (len(extent) - 1 - dim))
    return factor_of


def centred(own_key, dims, width, reach, shards=(), dtype=jnp.bfloat16):
    drawn = jax.random.normal(own_key, dims, jnp.float32) * width
    if len(shards) > 0:
        drawn = steps_of(own_key, dims, shards, -0.22, 0.18) * drawn
    return jnp.clip(drawn, min=-reach, max=reach).astype(dtype)


def bell_draw_with(own_key, dims, deviation, reach, split, heavy, kind=jnp.bfloat16):
    entries = deviation * jax.random.normal(own_key, dims, jnp.float32)
    if split:
        entries = entries * steps_of(own_key, dims, split, -0.22, 0.18)
    return jnp.clip(spiked(entries, jax.random.fold_in(own_key, 3), *heavy), -reach, reach).astype(kind)


def setup_inputs(seed: int = 0, part: int = 0) -> dict:
    splits = jax.random.split(jax.random.key(seed), 8)
    part_splits = jax.random.split(jax.random.fold_in(splits[7], part), 8)
    inputs = centred(part_splits[0], (TOKENS, D), 1.0, 6.0, ((0, 8), (1, 2)))
    gate_saved = centred(part_splits[1], (TOKENS, FF), 1.5, 8.0, ((0, 2), (1, 8)))
    up_saved = bell_draw_with(part_splits[2], (TOKENS, FF), 1.0, 6.0, ((0, 2), (1, 8)), (1, 0, 8, 2.0))
    cotangent = centred(part_splits[3], (TOKENS, D), 0.25, 2.0, ((0, 8), (1, 2)))
    gate_weight = centred(splits[4], (D, FF), D ** -0.5, 0.0625, ((0, 2), (1, 8)))
    up_weight = centred(splits[5], (D, FF), D ** -0.5, 0.0625, ((0, 2), (1, 8)))
    down_weight = centred(splits[6], (FF, D), FF ** -0.5, 0.046875, ((0, 8), (1, 2)))
    return {"inputs": inputs, "gate_saved": gate_saved, "up_saved": up_saved, "cotangent": cotangent, "gate_weight": gate_weight, "up_weight": up_weight, "down_weight": down_weight}


def reference(inputs, gate_saved, up_saved, cotangent, gate_weight, up_weight, down_weight):
    gvals = gate_saved.astype(jnp.float32)
    uvals = up_saved.astype(jnp.float32)
    sigma = jax.nn.sigmoid(gvals)
    hidden = (gvals * sigma * uvals).astype(jnp.bfloat16)
    grad_hidden = lax.dot_general(cotangent, down_weight, (((1,), (1,)), ((), ())), preferred_element_type=jnp.float32)
    grad_gate_act = (grad_hidden * uvals * sigma * (1.0 + gvals * (1.0 - sigma))).astype(jnp.bfloat16)
    grad_up_act = (grad_hidden * gvals * sigma).astype(jnp.bfloat16)
    contract_rows = (((0,), (0,)), ((), ()))
    grad_down = lax.dot_general(hidden, cotangent, contract_rows, preferred_element_type=jnp.float32).astype(jnp.bfloat16)
    grad_gate = lax.dot_general(inputs, grad_gate_act, contract_rows, preferred_element_type=jnp.float32).astype(jnp.bfloat16)
    grad_up = lax.dot_general(inputs, grad_up_act, contract_rows, preferred_element_type=jnp.float32).astype(jnp.bfloat16)
    contract_cols = (((1,), (1,)), ((), ()))
    total = lax.dot_general(grad_gate_act, gate_weight, contract_cols, preferred_element_type=jnp.float32)
    total = total + lax.dot_general(grad_up_act, up_weight, contract_cols, preferred_element_type=jnp.float32)
    grad_inputs = total.astype(jnp.bfloat16)
    return grad_inputs, grad_gate, grad_up, grad_down
```

```python
import jax
import jax.numpy as jnp
from jax import lax
from jax.experimental import pallas as pl
from jax.experimental.pallas import tpu as pltpu
from jax.sharding import PartitionSpec as P

ROWS = (((0,), (0,)), ((), ()))
COLS = (((1,), (1,)), ((), ()))


def swiglu_back(gate_vals, up_vals, grad_hidden):
    gvals = gate_vals.astype(jnp.float32)
    uvals = up_vals.astype(jnp.float32)
    sigma = jax.nn.sigmoid(gvals)
    hidden = (gvals * sigma * uvals).astype(jnp.bfloat16)
    grad_gate_act = (grad_hidden * uvals * sigma * (1.0 + gvals * (1.0 - sigma))).astype(
        jnp.bfloat16
    )
    grad_up_act = (grad_hidden * gvals * sigma).astype(jnp.bfloat16)
    return (hidden, grad_gate_act, grad_up_act)


def weight_grads_kernel(n_right, left_ref, *refs):
    left = left_ref[...].T
    for right_ref, out_ref in zip(refs[:n_right], refs[n_right:]):
        out_ref[...] = jnp.dot(
            left, right_ref[...], preferred_element_type=jnp.float32
        ).astype(jnp.bfloat16)


def weight_grads(left, rights, blocks):
    tokens, m = left.shape
    bm = m // blocks
    kern = lambda *refs: weight_grads_kernel(len(rights), *refs)
    n = rights[0].shape[1]
    return pl.pallas_call(
        kern,
        grid=(blocks,),
        in_specs=[pl.BlockSpec((tokens, bm), lambda i: (0, i))]
        + [pl.BlockSpec((tokens, n), lambda i: (0, 0)) for _ in rights],
        out_specs=[pl.BlockSpec((bm, n), lambda i: (i, 0)) for _ in rights],
        out_shape=[jax.ShapeDtypeStruct((m, n), jnp.bfloat16) for _ in rights],
        cost_estimate=pl.CostEstimate(
            flops=2 * tokens * m * n * len(rights),
            bytes_accessed=2 * (tokens * m + (tokens * n + m * n) * len(rights)),
            transcendentals=0,
        ),
        compiler_params=pltpu.CompilerParams(vmem_limit_bytes=56 * 2**20),
    )(left, *rights)


def per_device(inputs, gate_saved, up_saved, cotangent, gate_weight, up_weight, down_weight):
    cotan_all = lax.all_gather(cotangent, "row", axis=0, tiled=True)
    partial_hidden = lax.dot_general(
        cotan_all, down_weight, COLS, preferred_element_type=jnp.float32
    )
    gates_all, ups_all = (
        lax.all_gather(gate_saved, "col", axis=0, tiled=True),
        lax.all_gather(up_saved, "col", axis=0, tiled=True),
    )
    summed = lax.psum(partial_hidden, "col")
    hidden, grad_g, grad_u = swiglu_back(gates_all, ups_all, summed)
    total = lax.dot_general(grad_g, gate_weight, COLS, preferred_element_type=jnp.float32)
    total = total + lax.dot_general(grad_u, up_weight, COLS, preferred_element_type=jnp.float32)
    grad_inputs = lax.psum_scatter(total, "row", scatter_dimension=0, tiled=True).astype(
        jnp.bfloat16
    )
    inputs_all = lax.all_gather(inputs, "row", axis=0, tiled=True)
    (grad_down,) = weight_grads(hidden, (cotan_all,), max(1, hidden.shape[1] // 256))
    grad_gate, grad_up = weight_grads(inputs_all, (grad_g, grad_u), 8)
    return (grad_inputs, grad_gate, grad_up, grad_down)


def solution(mesh):
    return jax.shard_map(
        per_device,
        mesh=mesh,
        in_specs=(
            P(("groups", "row"), "col"),
            P(("groups", "col"), "row"),
            P(("groups", "col"), "row"),
            P(("groups", "row"), "col"),
            P("col", "row"),
            P("col", "row"),
            P("row", "col"),
        ),
        out_specs=(
            P(("groups", "row"), "col"),
            P(("groups", "col"), "row"),
            P(("groups", "col"), "row"),
            P(("groups", "row"), "col"),
        ),
        check_vma=False,
    )
```

```python
import functools

import jax
import jax.numpy as jnp
from jax import lax
from jax.experimental import pallas as pl
from jax.experimental.pallas import tpu as pltpu
from jax.sharding import PartitionSpec as P

ROWS = (((0,), (0,)), ((), ()))
COLS = (((1,), (1,)), ((), ()))


def swiglu_back(gate_vals, up_vals, grad_hidden):
    gvals = gate_vals.astype(jnp.float32)
    uvals = up_vals.astype(jnp.float32)
    sigma = jax.nn.sigmoid(gvals)
    hidden = (gvals * sigma * uvals).astype(jnp.bfloat16)
    grad_gate_act = (grad_hidden * uvals * sigma * (1.0 + gvals * (1.0 - sigma))).astype(
        jnp.bfloat16
    )
    grad_up_act = (grad_hidden * gvals * sigma).astype(jnp.bfloat16)
    return (hidden, grad_gate_act, grad_up_act)


def weight_grads_kernel(n_right, left_ref, *refs):
    left = left_ref[...].T
    for right_ref, out_ref in zip(refs[:n_right], refs[n_right:]):
        out_ref[...] = jnp.dot(
            left, right_ref[...], preferred_element_type=jnp.float32
        ).astype(jnp.bfloat16)


def weight_grads(left, rights, blocks):
    tokens, m = left.shape
    bm = m // blocks
    kern = lambda *refs: weight_grads_kernel(len(rights), *refs)
    n = rights[0].shape[1]
    return pl.pallas_call(
        kern,
        grid=(blocks,),
        in_specs=[pl.BlockSpec((tokens, bm), lambda i: (0, i))]
        + [pl.BlockSpec((tokens, n), lambda i: (0, 0)) for _ in rights],
        out_specs=[pl.BlockSpec((bm, n), lambda i: (i, 0)) for _ in rights],
        out_shape=[jax.ShapeDtypeStruct((m, n), jnp.bfloat16) for _ in rights],
        cost_estimate=pl.CostEstimate(
            flops=2 * tokens * m * n * len(rights),
            bytes_accessed=2 * (tokens * m + (tokens * n + m * n) * len(rights)),
            transcendentals=0,
        ),
        compiler_params=pltpu.CompilerParams(vmem_limit_bytes=56 * 2**20),
    )(left, *rights)


def plain(inputs, gate_saved, up_saved, cotangent, gate_weight, up_weight, down_weight):
    cotan_all = lax.all_gather(cotangent, "row", axis=0, tiled=True)
    partial_hidden = lax.dot_general(
        cotan_all, down_weight, COLS, preferred_element_type=jnp.float32
    )
    gates_all, ups_all = (
        lax.all_gather(gate_saved, "col", axis=0, tiled=True),
        lax.all_gather(up_saved, "col", axis=0, tiled=True),
    )
    summed = lax.psum(partial_hidden, "col")
    hidden, grad_g, grad_u = swiglu_back(gates_all, ups_all, summed)
    total = lax.dot_general(grad_g, gate_weight, COLS, preferred_element_type=jnp.float32)
    total = total + lax.dot_general(grad_u, up_weight, COLS, preferred_element_type=jnp.float32)
    grad_inputs = lax.psum_scatter(total, "row", scatter_dimension=0, tiled=True).astype(
        jnp.bfloat16
    )
    inputs_all = lax.all_gather(inputs, "row", axis=0, tiled=True)
    (grad_down,) = weight_grads(hidden, (cotan_all,), max(1, hidden.shape[1] // 256))
    grad_gate, grad_up = weight_grads(inputs_all, (grad_g, grad_u), 8)
    return (grad_inputs, grad_gate, grad_up, grad_down)


MESH = pl.DeviceIdType.MESH


def lines_of(rows):
    across = 1
    while (2 * across) ** 3 <= rows:
        across *= 2
    return rows // across, across


class Place:
    def __init__(self, rows):
        self.deep, self.across = lines_of(rows)
        self.me = lax.axis_index("row")
        self.z, self.x = self.me // self.across, lax.rem(self.me, self.across)

    def z_at(self, d):
        return lax.rem(self.z + d + self.deep, self.deep)

    def x_at(self, e):
        return lax.rem(self.x + e + self.across, self.across)

    def row(self, z, x):
        return z * self.across + x

    def greet(self, col_too):
        barrier = pltpu.get_barrier_semaphore()
        others = [{"row": self.row(self.z_at(d), self.x)} for d in range(1, self.deep)]
        others += [{"row": self.row(self.z, self.x_at(e))} for e in range(1, self.across)]
        if col_too:
            others.append({"col": 1 - lax.axis_index("col")})
        for other in others:
            pl.semaphore_signal(barrier, inc=1, device_id=other, device_id_type=MESH)
        pl.semaphore_wait(barrier, len(others))


class Gather:
    def __init__(self, place, own, held, z_send, z_recv, x_send, x_recv):
        self.p, self.own, self.held = place, own, held
        self.sems = z_send, z_recv, x_send, x_recv

    def z_copy(self, d, row, src=None):
        p = self.p
        return pltpu.make_async_remote_copy(
            src_ref=self.held.at[row] if src is None else src,
            dst_ref=self.held.at[row],
            send_sem=self.sems[0].at[d - 1],
            recv_sem=self.sems[1].at[d - 1],
            device_id={"row": p.row(p.z_at(d), p.x)},
            device_id_type=MESH,
        )

    def x_copy(self, d, e, row, src=None):
        p = self.p
        return pltpu.make_async_remote_copy(
            src_ref=self.held.at[row] if src is None else src,
            dst_ref=self.held.at[row],
            send_sem=self.sems[2].at[d, e - 1],
            recv_sem=self.sems[3].at[d, e - 1],
            device_id={"row": p.row(p.z, p.x_at(e))},
            device_id_type=MESH,
        )

    def start(self):
        p = self.p
        for d in range(1, p.deep):
            self.z_copy(d, p.me, self.own).start()
        for e in range(1, p.across):
            self.x_copy(0, e, p.me, self.own).start()

    def forward(self, d):
        p = self.p
        row = p.row(p.z_at(-d), p.x)
        self.z_copy(d, row).wait_recv()
        for e in range(1, p.across):
            self.x_copy(d, e, row).start()

    def group(self, d):
        p = self.p
        for e in range(1, p.across):
            self.x_copy(d, e, p.row(p.z_at(-d), p.x_at(-e))).wait_recv()

    def finish(self):
        p = self.p
        for d in range(1, p.deep):
            self.z_copy(d, p.me, self.own).wait_send()
        for d in range(p.deep):
            row = p.row(p.z_at(-d), p.x)
            for e in range(1, p.across):
                self.x_copy(d, e, row).wait_send()


def gather_sems(rows):
    deep, across = lines_of(rows)
    dma = pltpu.SemaphoreType.DMA
    line, cross = (deep - 1,), (deep, across - 1)
    return [dma(line), dma(line), dma(cross), dma(cross)]


def hidden_kernel(
    rows, tile, cot_ref, gate_ref, up_ref, down_ref,
    cot_out, hidden_ref, gg_ref, gu_ref,
    down, held, part, theirs, gates, ups,
    z_send, z_recv, x_send, x_recv, p_send, p_recv, s_send, s_recv, local,
):
    p = Place(rows)
    col = lax.axis_index("col")
    deep, half = p.deep, p.deep // 2
    size = p.across * cot_ref.shape[0]
    depth, ff = cot_ref.shape[1], down_ref.shape[0]
    get_own = pltpu.make_async_copy(cot_ref, held.at[p.me], local.at[0])
    get_down = pltpu.make_async_copy(down_ref, down, local.at[1])
    mine = pl.ds(col * half, half)
    get_gate = pltpu.make_async_copy(gate_ref, gates.at[mine], local.at[2])
    get_up = pltpu.make_async_copy(up_ref, ups.at[mine], local.at[3])
    get_own.start()
    get_down.start()
    get_gate.start()
    get_up.start()
    p.greet(True)

    def saved(n, src, dst, at):
        return pltpu.make_async_remote_copy(
            src_ref=src, dst_ref=dst.at[pl.ds(at * half, half)],
            send_sem=s_send.at[n], recv_sem=s_recv.at[n],
            device_id={"col": 1 - col}, device_id_type=MESH,
        )

    def share(d):
        return pltpu.make_async_remote_copy(
            src_ref=part.at[d], dst_ref=theirs.at[d],
            send_sem=p_send.at[d], recv_sem=p_recv.at[d],
            device_id={"col": 1 - col}, device_id_type=MESH,
        )

    gather = Gather(p, cot_ref, held, z_send, z_recv, x_send, x_recv)
    gather.start()
    saved(0, gate_ref, gates, col).start()
    saved(1, up_ref, ups, col).start()
    get_own.wait()
    get_down.wait()

    def activations(d):
        z = p.z_at(-d)
        share(d).wait_recv()

        def some(i, carry):
            at = pl.ds(pl.multiple_of(i * 16, 16), 16)
            outs = swiglu_back(gates[z, at, :], ups[z, at, :], part[d, at, :] + theirs[d, at, :])
            for ref, value in zip((hidden_ref, gg_ref, gu_ref), outs):
                ref[z, at, :] = value
            return carry

        lax.fori_loop(0, size // 16, some, 0)

    for d in range(deep):
        z = p.z_at(-d)
        if d > 0:
            gather.forward(d)
        gather.group(d)
        left = held[pl.ds(z * p.across, p.across)].reshape(size, depth)

        def some(j, carry):
            at = pl.ds(pl.multiple_of(j * tile, tile), tile)
            part[d, :, at] = lax.dot_general(
                left, down[at, :], COLS, preferred_element_type=jnp.float32
            )
            return carry

        lax.fori_loop(0, ff // tile, some, 0)
        share(d).start()
        if d == 0:
            get_gate.wait()
            get_up.wait()
            saved(0, gate_ref, gates, 1 - col).wait_recv()
            saved(1, up_ref, ups, 1 - col).wait_recv()
        else:
            activations(d - 1)
    put = pltpu.make_async_copy(held, cot_out, local.at[0])
    put.start()
    activations(deep - 1)
    gather.finish()
    saved(0, gate_ref, gates, col).wait_send()
    saved(1, up_ref, ups, col).wait_send()
    for d in range(deep):
        share(d).wait_send()
    put.wait()


def inputs_kernel(
    rows, tile, in_ref, gg_ref, gu_ref, gate_ref, up_ref,
    in_out, out_ref,
    gate, up, tot, own, to_x, from_x, to_z, from_z,
    z_send, z_recv, x_send, x_recv, rx_send, rx_recv, rz_send, rz_recv, local,
):
    p = Place(rows)
    deep, across = p.deep, p.across
    tok, depth = in_ref.shape
    get_gate = pltpu.make_async_copy(gate_ref, gate, local.at[0])
    get_up = pltpu.make_async_copy(up_ref, up, local.at[1])
    put_own = pltpu.make_async_copy(in_ref, in_out.at[p.me], local.at[2])
    get_gate.start()
    get_up.start()
    put_own.start()
    p.greet(False)
    gather = Gather(p, in_ref, in_out, z_send, z_recv, x_send, x_recv)
    gather.start()

    def over_x(d, e):
        return pltpu.make_async_remote_copy(
            src_ref=to_x.at[d, e - 1], dst_ref=from_x.at[d, e - 1],
            send_sem=rx_send.at[d, e - 1], recv_sem=rx_recv.at[d, e - 1],
            device_id={"row": p.row(p.z, p.x_at(e))}, device_id_type=MESH,
        )

    def over_z(d):
        return pltpu.make_async_remote_copy(
            src_ref=to_z.at[d - 1], dst_ref=from_z.at[d - 1],
            send_sem=rz_send.at[d - 1], recv_sem=rz_recv.at[d - 1],
            device_id={"row": p.row(p.z_at(d), p.x)}, device_id_type=MESH,
        )

    def columns(step):
        def some(j, carry):
            step(pl.ds(pl.multiple_of(j * tile, tile), tile))
            return carry

        lax.fori_loop(0, depth // tile, some, 0)

    def along_x(d, at):
        total = own[d, :, at]
        for e in range(1, across):
            total += from_x[d, e - 1, :, at].astype(jnp.float32)
        return total

    def pass_on(d):
        for e in range(1, across):
            over_x(d, e).wait_recv()

        def step(at):
            to_z[d - 1, :, at] = along_x(d, at).astype(jnp.bfloat16)

        columns(step)
        over_z(d).start()

    get_gate.wait()
    get_up.wait()
    put_own.wait()
    order = list(range(1, deep)) + [0]
    for n, d in enumerate(order):
        z = p.z_at(d)

        def step(at):
            total = lax.dot_general(
                gg_ref[z], gate[at, :], COLS, preferred_element_type=jnp.float32
            ) + lax.dot_general(gu_ref[z], up[at, :], COLS, preferred_element_type=jnp.float32)
            tot[...] = total.reshape(across, tok, tile)
            own[d, :, at] = tot[p.x]
            for e in range(1, across):
                to_x[d, e - 1, :, at] = tot[p.x_at(e)].astype(jnp.bfloat16)

        columns(step)
        for e in range(1, across):
            over_x(d, e).start()
        if n > 0:
            pass_on(order[n - 1])
            gather.forward(n)
    for d in range(deep):
        gather.group(d)
    for e in range(1, across):
        over_x(0, e).wait_recv()
    for d in range(1, deep):
        over_z(d).wait_recv()

    def step(at):
        total = along_x(0, at)
        for d in range(1, deep):
            total += from_z[d - 1, :, at].astype(jnp.float32)
        out_ref[:, at] = total.astype(jnp.bfloat16)

    columns(step)
    gather.finish()
    for d in range(deep):
        for e in range(1, across):
            over_x(d, e).wait_send()
    for d in range(1, deep):
        over_z(d).wait_send()


def per_device(inputs, gate_saved, up_saved, cotangent, gate_weight, up_weight, down_weight):
    rows, cols = lax.axis_size("row"), lax.axis_size("col")
    deep, across = lines_of(rows)
    tok, depth = cotangent.shape
    ff = down_weight.shape[0]
    size = tok * across
    if cols != 2 or tok % 16 or deep % 2 or across < 2 or ff % 256 or depth % 256:
        return plain(
            inputs, gate_saved, up_saved, cotangent, gate_weight, up_weight, down_weight
        )
    bf16, f32 = jnp.bfloat16, jnp.float32
    dma, shape = pltpu.SemaphoreType.DMA, jax.ShapeDtypeStruct
    vmem, anywhere = pl.BlockSpec(memory_space=pltpu.VMEM), pl.BlockSpec(memory_space=pl.ANY)
    tile = 256 if ff % 512 or depth % 512 else 512
    halves = (deep // 2, size, ff)
    cot_all, hidden, gg, gu = pl.pallas_call(
        functools.partial(hidden_kernel, rows, tile),
        in_specs=[anywhere] * 4,
        out_specs=[anywhere, vmem, vmem, vmem],
        out_shape=[shape((rows, tok, depth), bf16)] + [shape((deep, size, ff), bf16)] * 3,
        scratch_shapes=[
            pltpu.VMEM((ff, depth), bf16),
            pltpu.VMEM((rows, tok, depth), bf16),
            pltpu.VMEM((deep, size, ff), f32),
            pltpu.VMEM((deep, size, ff), f32),
            pltpu.VMEM((deep, size, ff), bf16),
            pltpu.VMEM((deep, size, ff), bf16),
            *gather_sems(rows),
            dma((deep,)), dma((deep,)), dma((2,)), dma((2,)), dma((4,)),
        ],
        cost_estimate=pl.CostEstimate(
            flops=2 * rows * tok * depth * ff, bytes_accessed=2 * ff * depth, transcendentals=0
        ),
        compiler_params=pltpu.CompilerParams(
            collective_id=0, has_side_effects=True, vmem_limit_bytes=58 * 2**20
        ),
    )(cotangent, gate_saved.reshape(halves), up_saved.reshape(halves), down_weight)
    inputs_all, grad_inputs = pl.pallas_call(
        functools.partial(inputs_kernel, rows, tile),
        in_specs=[anywhere, vmem, vmem, anywhere, anywhere],
        out_specs=[anywhere, vmem],
        out_shape=[shape((rows, tok, depth), bf16), shape((tok, depth), bf16)],
        scratch_shapes=[
            pltpu.VMEM((depth, ff), bf16),
            pltpu.VMEM((depth, ff), bf16),
            pltpu.VMEM((across, tok, tile), f32),
            pltpu.VMEM((deep, tok, depth), f32),
            pltpu.VMEM((deep, across - 1, tok, depth), bf16),
            pltpu.VMEM((deep, across - 1, tok, depth), bf16),
            pltpu.VMEM((deep - 1, tok, depth), bf16),
            pltpu.VMEM((deep - 1, tok, depth), bf16),
            *gather_sems(rows),
            *gather_sems(rows)[2:],
            *gather_sems(rows)[:2],
            dma((3,)),
        ],
        cost_estimate=pl.CostEstimate(
            flops=4 * rows * tok * depth * ff, bytes_accessed=4 * ff * depth, transcendentals=0
        ),
        compiler_params=pltpu.CompilerParams(
            collective_id=1, has_side_effects=True, vmem_limit_bytes=58 * 2**20
        ),
    )(inputs, gg, gu, gate_weight, up_weight)
    flat = lambda a: a.reshape(-1, a.shape[-1])
    (grad_down,) = weight_grads(flat(hidden), (flat(cot_all),), max(1, ff // 256))
    grad_gate, grad_up = weight_grads(flat(inputs_all), (flat(gg), flat(gu)), 8)
    return (grad_inputs, grad_gate, grad_up, grad_down)


def solution(mesh):
    return jax.shard_map(
        per_device,
        mesh=mesh,
        in_specs=(
            P(("groups", "row"), "col"),
            P(("groups", "col"), "row"),
            P(("groups", "col"), "row"),
            P(("groups", "row"), "col"),
            P("col", "row"),
            P("col", "row"),
            P("row", "col"),
        ),
        out_specs=(
            P(("groups", "row"), "col"),
            P(("groups", "col"), "row"),
            P(("groups", "col"), "row"),
            P(("groups", "row"), "col"),
        ),
        check_vma=False,
    )
```

```python
import functools

import jax
import jax.numpy as jnp
from jax import lax
from jax.experimental import pallas as pl
from jax.experimental.pallas import tpu as pltpu
from jax.sharding import PartitionSpec as P

ROWS = (((0,), (0,)), ((), ()))
COLS = (((1,), (1,)), ((), ()))


def swiglu_back(gate_vals, up_vals, grad_hidden):
    gvals = gate_vals.astype(jnp.float32)
    uvals = up_vals.astype(jnp.float32)
    sigma = jax.nn.sigmoid(gvals)
    hidden = (gvals * sigma * uvals).astype(jnp.bfloat16)
    grad_gate_act = (grad_hidden * uvals * sigma * (1.0 + gvals * (1.0 - sigma))).astype(
        jnp.bfloat16
    )
    grad_up_act = (grad_hidden * gvals * sigma).astype(jnp.bfloat16)
    return (hidden, grad_gate_act, grad_up_act)


def weight_grads_kernel(n_right, left_ref, *refs):
    left = left_ref[...].T
    for right_ref, out_ref in zip(refs[:n_right], refs[n_right:]):
        out_ref[...] = jnp.dot(
            left, right_ref[...], preferred_element_type=jnp.float32
        ).astype(jnp.bfloat16)


def weight_grads(left, rights, blocks):
    tokens, m = left.shape
    bm = m // blocks
    kern = lambda *refs: weight_grads_kernel(len(rights), *refs)
    n = rights[0].shape[1]
    return pl.pallas_call(
        kern,
        grid=(blocks,),
        in_specs=[pl.BlockSpec((tokens, bm), lambda i: (0, i))]
        + [pl.BlockSpec((tokens, n), lambda i: (0, 0)) for _ in rights],
        out_specs=[pl.BlockSpec((bm, n), lambda i: (i, 0)) for _ in rights],
        out_shape=[jax.ShapeDtypeStruct((m, n), jnp.bfloat16) for _ in rights],
        cost_estimate=pl.CostEstimate(
            flops=2 * tokens * m * n * len(rights),
            bytes_accessed=2 * (tokens * m + (tokens * n + m * n) * len(rights)),
            transcendentals=0,
        ),
        compiler_params=pltpu.CompilerParams(vmem_limit_bytes=56 * 2**20),
    )(left, *rights)


def plain(inputs, gate_saved, up_saved, cotangent, gate_weight, up_weight, down_weight):
    cotan_all = lax.all_gather(cotangent, "row", axis=0, tiled=True)
    partial_hidden = lax.dot_general(
        cotan_all, down_weight, COLS, preferred_element_type=jnp.float32
    )
    gates_all, ups_all = (
        lax.all_gather(gate_saved, "col", axis=0, tiled=True),
        lax.all_gather(up_saved, "col", axis=0, tiled=True),
    )
    summed = lax.psum(partial_hidden, "col")
    hidden, grad_g, grad_u = swiglu_back(gates_all, ups_all, summed)
    total = lax.dot_general(grad_g, gate_weight, COLS, preferred_element_type=jnp.float32)
    total = total + lax.dot_general(grad_u, up_weight, COLS, preferred_element_type=jnp.float32)
    grad_inputs = lax.psum_scatter(total, "row", scatter_dimension=0, tiled=True).astype(
        jnp.bfloat16
    )
    inputs_all = lax.all_gather(inputs, "row", axis=0, tiled=True)
    (grad_down,) = weight_grads(hidden, (cotan_all,), max(1, hidden.shape[1] // 256))
    grad_gate, grad_up = weight_grads(inputs_all, (grad_g, grad_u), 8)
    return (grad_inputs, grad_gate, grad_up, grad_down)


MESH = pl.DeviceIdType.MESH


def lines_of(rows):
    across = 1
    while (2 * across) ** 3 <= rows:
        across *= 2
    return rows // across, across


class Place:
    def __init__(self, rows):
        self.deep, self.across = lines_of(rows)
        self.me = lax.axis_index("row")
        self.z, self.x = self.me // self.across, lax.rem(self.me, self.across)

    def z_at(self, d):
        return lax.rem(self.z + d + self.deep, self.deep)

    def x_at(self, e):
        return lax.rem(self.x + e + self.across, self.across)

    def row(self, z, x):
        return z * self.across + x

    def greet(self, col_too):
        barrier = pltpu.get_barrier_semaphore()
        others = [{"row": self.row(self.z_at(d), self.x)} for d in range(1, self.deep)]
        others += [{"row": self.row(self.z, self.x_at(e))} for e in range(1, self.across)]
        if col_too:
            others.append({"col": 1 - lax.axis_index("col")})
        for other in others:
            pl.semaphore_signal(barrier, inc=1, device_id=other, device_id_type=MESH)
        pl.semaphore_wait(barrier, len(others))


class Gather:
    def __init__(self, place, own, held, z_send, z_recv, x_send, x_recv):
        self.p, self.own, self.held = place, own, held
        self.sems = z_send, z_recv, x_send, x_recv

    def z_copy(self, d, row, src=None):
        p = self.p
        return pltpu.make_async_remote_copy(
            src_ref=self.held.at[row] if src is None else src,
            dst_ref=self.held.at[row],
            send_sem=self.sems[0].at[d - 1],
            recv_sem=self.sems[1].at[d - 1],
            device_id={"row": p.row(p.z_at(d), p.x)},
            device_id_type=MESH,
        )

    def x_copy(self, d, e, row, src=None):
        p = self.p
        return pltpu.make_async_remote_copy(
            src_ref=self.held.at[row] if src is None else src,
            dst_ref=self.held.at[row],
            send_sem=self.sems[2].at[d, e - 1],
            recv_sem=self.sems[3].at[d, e - 1],
            device_id={"row": p.row(p.z, p.x_at(e))},
            device_id_type=MESH,
        )

    def start(self):
        p = self.p
        for d in range(1, p.deep):
            self.z_copy(d, p.me, self.own).start()
        self.own_over_x()

    def own_over_x(self):
        for e in range(1, self.p.across):
            self.x_copy(0, e, self.p.me, self.own).start()

    def over_x(self, d):
        p = self.p
        for e in range(1, p.across):
            self.x_copy(d, e, p.row(p.z_at(-d), p.x)).start()

    def arrived(self, d):
        self.z_copy(d, self.p.row(self.p.z_at(-d), self.p.x)).wait_recv()

    def forward(self, d):
        self.arrived(d)
        self.over_x(d)

    def group(self, d):
        p = self.p
        for e in range(1, p.across):
            self.x_copy(d, e, p.row(p.z_at(-d), p.x_at(-e))).wait_recv()

    def finish(self, over_z, over_x):
        p = self.p
        for d in over_z:
            self.z_copy(d, p.me, self.own).wait_send()
        for d in over_x:
            row = p.row(p.z_at(-d), p.x)
            for e in range(1, p.across):
                self.x_copy(d, e, row).wait_send()


def gather_sems(rows):
    deep, across = lines_of(rows)
    dma = pltpu.SemaphoreType.DMA
    line, cross = (deep - 1,), (deep, across - 1)
    return [dma(line), dma(line), dma(cross), dma(cross)]


def hidden_kernel(
    rows, tile, cot_ref, in_ref, gate_ref, up_ref, down_ref,
    cot_out, in_out, hidden_ref, gg_ref, gu_ref,
    down, held, part, theirs, gates, ups,
    z_send, z_recv, x_send, x_recv, iz_send, iz_recv, ix_send, ix_recv,
    p_send, p_recv, s_send, s_recv, local,
):
    p = Place(rows)
    early = p.deep // 2
    col = lax.axis_index("col")
    deep, half = p.deep, p.deep // 2
    size = p.across * cot_ref.shape[0]
    depth, ff = cot_ref.shape[1], down_ref.shape[0]
    get_own = pltpu.make_async_copy(cot_ref, held.at[p.me], local.at[0])
    get_down = pltpu.make_async_copy(down_ref, down, local.at[1])
    mine = pl.ds(col * half, half)
    get_gate = pltpu.make_async_copy(gate_ref, gates.at[mine], local.at[2])
    get_up = pltpu.make_async_copy(up_ref, ups.at[mine], local.at[3])
    put_own = pltpu.make_async_copy(in_ref, in_out.at[p.me], local.at[4])
    get_own.start()
    get_down.start()
    put_own.start()
    get_gate.start()
    get_up.start()
    p.greet(True)

    def saved(n, src, dst, at):
        return pltpu.make_async_remote_copy(
            src_ref=src, dst_ref=dst.at[pl.ds(at * half, half)],
            send_sem=s_send.at[n], recv_sem=s_recv.at[n],
            device_id={"col": 1 - col}, device_id_type=MESH,
        )

    def share(d):
        return pltpu.make_async_remote_copy(
            src_ref=part.at[d], dst_ref=theirs.at[d],
            send_sem=p_send.at[d], recv_sem=p_recv.at[d],
            device_id={"col": 1 - col}, device_id_type=MESH,
        )

    gather = Gather(p, cot_ref, held, z_send, z_recv, x_send, x_recv)
    ins = Gather(p, in_ref, in_out, iz_send, iz_recv, ix_send, ix_recv)
    gather.start()
    saved(0, gate_ref, gates, col).start()
    saved(1, up_ref, ups, col).start()
    get_own.wait()
    get_down.wait()

    def activations(d):
        z = p.z_at(-d)
        share(d).wait_recv()

        def some(i, carry):
            at = pl.ds(pl.multiple_of(i * 16, 16), 16)
            outs = swiglu_back(gates[z, at, :], ups[z, at, :], part[d, at, :] + theirs[d, at, :])
            for ref, value in zip((hidden_ref, gg_ref, gu_ref), outs):
                ref[z, at, :] = value
            return carry

        lax.fori_loop(0, size // 16, some, 0)

    for d in range(deep):
        z = p.z_at(-d)
        if d + 1 < deep:
            gather.forward(d + 1)
            ins.z_copy(d + 1, p.me, in_ref).start()
        if d + 2 == deep:
            ins.own_over_x()
        gather.group(d)
        if d + 1 == deep:
            for n in range(1, early):
                ins.forward(n)
        left = held[pl.ds(z * p.across, p.across)].reshape(size, depth)

        def some(j, carry):
            at = pl.ds(pl.multiple_of(j * tile, tile), tile)
            part[d, :, at] = lax.dot_general(
                left, down[at, :], COLS, preferred_element_type=jnp.float32
            )
            return carry

        lax.fori_loop(0, ff // tile, some, 0)
        share(d).start()
        if d == 0:
            get_gate.wait()
            get_up.wait()
            saved(0, gate_ref, gates, 1 - col).wait_recv()
            saved(1, up_ref, ups, 1 - col).wait_recv()
        else:
            activations(d - 1)
    put = pltpu.make_async_copy(held, cot_out, local.at[0])
    put.start()
    activations(deep - 1)
    for d in range(early, deep):
        ins.arrived(d)
    for d in range(early):
        ins.group(d)
    gather.finish(range(1, deep), range(deep))
    ins.finish(range(1, deep), range(early))
    put_own.wait()
    saved(0, gate_ref, gates, col).wait_send()
    saved(1, up_ref, ups, col).wait_send()
    for d in range(deep):
        share(d).wait_send()
    put.wait()


def inputs_kernel(
    rows, tile, in_ref, gg_ref, gu_ref, gate_ref, up_ref,
    in_out, out_ref,
    gate, up, tot, own, to_x, from_x, to_z, from_z,
    x_send, x_recv, rx_send, rx_recv, rz_send, rz_recv, local,
):
    p = Place(rows)
    deep, across = p.deep, p.across
    late = range(deep // 2, deep)
    tok, depth = out_ref.shape

    def weights(j):
        at = pl.ds(pl.multiple_of(j * tile, tile), tile)
        return [
            pltpu.make_async_copy(ref.at[at, :], to.at[at, :], local.at[n, j])
            for n, (ref, to) in enumerate(((gate_ref, gate), (up_ref, up)))
        ]

    for j in range(depth // tile):
        for copy in weights(j):
            copy.start()
    p.greet(False)
    gather = Gather(p, None, in_out, None, None, x_send, x_recv)
    for d in late:
        gather.over_x(d)

    def over_x(d, e):
        return pltpu.make_async_remote_copy(
            src_ref=to_x.at[d, e - 1], dst_ref=from_x.at[d, e - 1],
            send_sem=rx_send.at[d, e - 1], recv_sem=rx_recv.at[d, e - 1],
            device_id={"row": p.row(p.z, p.x_at(e))}, device_id_type=MESH,
        )

    def over_z(d):
        return pltpu.make_async_remote_copy(
            src_ref=to_z.at[d - 1], dst_ref=from_z.at[d - 1],
            send_sem=rz_send.at[d - 1], recv_sem=rz_recv.at[d - 1],
            device_id={"row": p.row(p.z_at(d), p.x)}, device_id_type=MESH,
        )

    def columns(step):
        def some(j, carry):
            step(j, pl.ds(pl.multiple_of(j * tile, tile), tile))
            return carry

        lax.fori_loop(0, depth // tile, some, 0)

    def along_x(d, at):
        total = own[d, :, at]
        for e in range(1, across):
            total += from_x[d, e - 1, :, at].astype(jnp.float32)
        return total

    def pass_on(d):
        for e in range(1, across):
            over_x(d, e).wait_recv()

        def step(j, at):
            to_z[d - 1, :, at] = along_x(d, at).astype(jnp.bfloat16)

        columns(step)
        over_z(d).start()

    order = list(range(1, deep)) + [0]
    for n, d in enumerate(order):
        z = p.z_at(d)

        def step(j, at):
            if n == 0:
                for copy in weights(j):
                    copy.wait()
            total = lax.dot_general(
                gg_ref[z], gate[at, :], COLS, preferred_element_type=jnp.float32
            ) + lax.dot_general(gu_ref[z], up[at, :], COLS, preferred_element_type=jnp.float32)
            tot[...] = total.reshape(across, tok, tile)
            own[d, :, at] = tot[p.x]
            for e in range(1, across):
                to_x[d, e - 1, :, at] = tot[p.x_at(e)].astype(jnp.bfloat16)

        columns(step)
        for e in range(1, across):
            over_x(d, e).start()
    for d in range(1, deep):
        pass_on(d)
    for e in range(1, across):
        over_x(0, e).wait_recv()
    for d in range(1, deep):
        over_z(d).wait_recv()

    def step(j, at):
        total = along_x(0, at)
        for d in range(1, deep):
            total += from_z[d - 1, :, at].astype(jnp.float32)
        out_ref[:, at] = total.astype(jnp.bfloat16)

    columns(step)
    for d in late:
        gather.group(d)
    gather.finish((), late)
    for d in range(deep):
        for e in range(1, across):
            over_x(d, e).wait_send()
    for d in range(1, deep):
        over_z(d).wait_send()


def per_device(inputs, gate_saved, up_saved, cotangent, gate_weight, up_weight, down_weight):
    rows, cols = lax.axis_size("row"), lax.axis_size("col")
    deep, across = lines_of(rows)
    tok, depth = cotangent.shape
    ff = down_weight.shape[0]
    size = tok * across
    if cols != 2 or tok % 16 or deep % 2 or across < 2 or ff % 256 or depth % 256:
        return plain(
            inputs, gate_saved, up_saved, cotangent, gate_weight, up_weight, down_weight
        )
    bf16, f32 = jnp.bfloat16, jnp.float32
    dma, shape = pltpu.SemaphoreType.DMA, jax.ShapeDtypeStruct
    vmem, anywhere = pl.BlockSpec(memory_space=pltpu.VMEM), pl.BlockSpec(memory_space=pl.ANY)
    tile = 256 if ff % 512 or depth % 512 else 512
    halves = (deep // 2, size, ff)
    cot_all, inputs_some, hidden, gg, gu = pl.pallas_call(
        functools.partial(hidden_kernel, rows, tile),
        in_specs=[anywhere] * 5,
        out_specs=[anywhere, anywhere, vmem, vmem, vmem],
        out_shape=[shape((rows, tok, depth), bf16)] * 2 + [shape((deep, size, ff), bf16)] * 3,
        scratch_shapes=[
            pltpu.VMEM((ff, depth), bf16),
            pltpu.VMEM((rows, tok, depth), bf16),
            pltpu.VMEM((deep, size, ff), f32),
            pltpu.VMEM((deep, size, ff), f32),
            pltpu.VMEM((deep, size, ff), bf16),
            pltpu.VMEM((deep, size, ff), bf16),
            *gather_sems(rows),
            *gather_sems(rows),
            dma((deep,)), dma((deep,)), dma((2,)), dma((2,)), dma((5,)),
        ],
        cost_estimate=pl.CostEstimate(
            flops=2 * rows * tok * depth * ff, bytes_accessed=2 * ff * depth, transcendentals=0
        ),
        compiler_params=pltpu.CompilerParams(
            collective_id=0, has_side_effects=True, vmem_limit_bytes=58 * 2**20
        ),
    )(cotangent, inputs, gate_saved.reshape(halves), up_saved.reshape(halves), down_weight)
    inputs_all, grad_inputs = pl.pallas_call(
        functools.partial(inputs_kernel, rows, tile),
        in_specs=[anywhere, vmem, vmem, anywhere, anywhere],
        out_specs=[anywhere, vmem],
        out_shape=[shape((rows, tok, depth), bf16), shape((tok, depth), bf16)],
        scratch_shapes=[
            pltpu.VMEM((depth, ff), bf16),
            pltpu.VMEM((depth, ff), bf16),
            pltpu.VMEM((across, tok, tile), f32),
            pltpu.VMEM((deep, tok, depth), f32),
            pltpu.VMEM((deep, across - 1, tok, depth), bf16),
            pltpu.VMEM((deep, across - 1, tok, depth), bf16),
            pltpu.VMEM((deep - 1, tok, depth), bf16),
            pltpu.VMEM((deep - 1, tok, depth), bf16),
            *gather_sems(rows)[2:],
            *gather_sems(rows)[2:],
            *gather_sems(rows)[:2],
            dma((2, depth // tile)),
        ],
        input_output_aliases={0: 0},
        cost_estimate=pl.CostEstimate(
            flops=4 * rows * tok * depth * ff, bytes_accessed=4 * ff * depth, transcendentals=0
        ),
        compiler_params=pltpu.CompilerParams(
            collective_id=1, has_side_effects=True, vmem_limit_bytes=58 * 2**20
        ),
    )(inputs_some, gg, gu, gate_weight, up_weight)
    flat = lambda a: a.reshape(-1, a.shape[-1])
    (grad_down,) = weight_grads(flat(hidden), (flat(cot_all),), max(1, ff // 256))
    grad_gate, grad_up = weight_grads(flat(inputs_all), (flat(gg), flat(gu)), 8)
    return (grad_inputs, grad_gate, grad_up, grad_down)


def solution(mesh):
    return jax.shard_map(
        per_device,
        mesh=mesh,
        in_specs=(
            P(("groups", "row"), "col"),
            P(("groups", "col"), "row"),
            P(("groups", "col"), "row"),
            P(("groups", "row"), "col"),
            P("col", "row"),
            P("col", "row"),
            P("row", "col"),
        ),
        out_specs=(
            P(("groups", "row"), "col"),
            P(("groups", "col"), "row"),
            P(("groups", "col"), "row"),
            P(("groups", "row"), "col"),
        ),
        check_vma=False,
    )
```

```python
import functools

import jax
import jax.numpy as jnp
from jax import lax
from jax.experimental import pallas as pl
from jax.experimental.pallas import tpu as pltpu
from jax.sharding import PartitionSpec as P

ROWS = (((0,), (0,)), ((), ()))
COLS = (((1,), (1,)), ((), ()))


def swiglu_back(gate_vals, up_vals, grad_hidden):
    gvals = gate_vals.astype(jnp.float32)
    uvals = up_vals.astype(jnp.float32)
    sigma = jax.nn.sigmoid(gvals)
    hidden = (gvals * sigma * uvals).astype(jnp.bfloat16)
    grad_gate_act = (grad_hidden * uvals * sigma * (1.0 + gvals * (1.0 - sigma))).astype(
        jnp.bfloat16
    )
    grad_up_act = (grad_hidden * gvals * sigma).astype(jnp.bfloat16)
    return (hidden, grad_gate_act, grad_up_act)


def weight_grads_kernel(n_right, left_ref, *refs):
    left = left_ref[...].T
    for right_ref, out_ref in zip(refs[:n_right], refs[n_right:]):
        out_ref[...] = jnp.dot(
            left, right_ref[...], preferred_element_type=jnp.float32
        ).astype(jnp.bfloat16)


def weight_grads(left, rights, blocks):
    tokens, m = left.shape
    bm = m // blocks
    kern = lambda *refs: weight_grads_kernel(len(rights), *refs)
    n = rights[0].shape[1]
    return pl.pallas_call(
        kern,
        grid=(blocks,),
        in_specs=[pl.BlockSpec((tokens, bm), lambda i: (0, i))]
        + [pl.BlockSpec((tokens, n), lambda i: (0, 0)) for _ in rights],
        out_specs=[pl.BlockSpec((bm, n), lambda i: (i, 0)) for _ in rights],
        out_shape=[jax.ShapeDtypeStruct((m, n), jnp.bfloat16) for _ in rights],
        cost_estimate=pl.CostEstimate(
            flops=2 * tokens * m * n * len(rights),
            bytes_accessed=2 * (tokens * m + (tokens * n + m * n) * len(rights)),
            transcendentals=0,
        ),
        compiler_params=pltpu.CompilerParams(vmem_limit_bytes=56 * 2**20),
    )(left, *rights)


def plain(inputs, gate_saved, up_saved, cotangent, gate_weight, up_weight, down_weight):
    cotan_all = lax.all_gather(cotangent, "row", axis=0, tiled=True)
    partial_hidden = lax.dot_general(
        cotan_all, down_weight, COLS, preferred_element_type=jnp.float32
    )
    gates_all, ups_all = (
        lax.all_gather(gate_saved, "col", axis=0, tiled=True),
        lax.all_gather(up_saved, "col", axis=0, tiled=True),
    )
    summed = lax.psum(partial_hidden, "col")
    hidden, grad_g, grad_u = swiglu_back(gates_all, ups_all, summed)
    total = lax.dot_general(grad_g, gate_weight, COLS, preferred_element_type=jnp.float32)
    total = total + lax.dot_general(grad_u, up_weight, COLS, preferred_element_type=jnp.float32)
    grad_inputs = lax.psum_scatter(total, "row", scatter_dimension=0, tiled=True).astype(
        jnp.bfloat16
    )
    inputs_all = lax.all_gather(inputs, "row", axis=0, tiled=True)
    (grad_down,) = weight_grads(hidden, (cotan_all,), max(1, hidden.shape[1] // 256))
    grad_gate, grad_up = weight_grads(inputs_all, (grad_g, grad_u), 8)
    return (grad_inputs, grad_gate, grad_up, grad_down)


MESH = pl.DeviceIdType.MESH


def lines_of(rows):
    across = 1
    while (2 * across) ** 3 <= rows:
        across *= 2
    return rows // across, across


def steps_of(deep):
    return [0, 1] + ([deep - 1] if deep > 2 else []) + list(range(2, deep - 1))


class Place:
    def __init__(self, rows):
        self.deep, self.across = lines_of(rows)
        self.me = lax.axis_index("row")
        self.z, self.x = self.me // self.across, lax.rem(self.me, self.across)

    def z_at(self, d):
        return lax.rem(self.z + d + self.deep, self.deep)

    def x_at(self, e):
        return lax.rem(self.x + e + self.across, self.across)

    def row(self, z, x):
        return z * self.across + x

    def greet(self, col_too):
        barrier = pltpu.get_barrier_semaphore()
        others = [{"row": self.row(self.z_at(d), self.x)} for d in range(1, self.deep)]
        others += [{"row": self.row(self.z, self.x_at(e))} for e in range(1, self.across)]
        if col_too:
            others.append({"col": 1 - lax.axis_index("col")})
        for other in others:
            pl.semaphore_signal(barrier, inc=1, device_id=other, device_id_type=MESH)
        pl.semaphore_wait(barrier, len(others))


class Gather:
    def __init__(self, place, own, held, z_send, z_recv, x_send, x_recv):
        self.p, self.own, self.held = place, own, held
        self.sems = z_send, z_recv, x_send, x_recv

    def z_copy(self, d, row, src=None):
        p = self.p
        return pltpu.make_async_remote_copy(
            src_ref=self.held.at[row] if src is None else src,
            dst_ref=self.held.at[row],
            send_sem=self.sems[0].at[d - 1],
            recv_sem=self.sems[1].at[d - 1],
            device_id={"row": p.row(p.z_at(d), p.x)},
            device_id_type=MESH,
        )

    def x_copy(self, d, e, row, src=None):
        p = self.p
        return pltpu.make_async_remote_copy(
            src_ref=self.held.at[row] if src is None else src,
            dst_ref=self.held.at[row],
            send_sem=self.sems[2].at[d, e - 1],
            recv_sem=self.sems[3].at[d, e - 1],
            device_id={"row": p.row(p.z, p.x_at(e))},
            device_id_type=MESH,
        )

    def along_z(self, d):
        self.z_copy(d, self.p.me, self.own).start()

    def own_over_x(self):
        for e in range(1, self.p.across):
            self.x_copy(0, e, self.p.me, self.own).start()

    def over_x(self, d):
        p = self.p
        for e in range(1, p.across):
            self.x_copy(d, e, p.row(p.z_at(-d), p.x)).start()

    def arrived(self, d):
        self.z_copy(d, self.p.row(self.p.z_at(-d), self.p.x)).wait_recv()

    def group(self, d):
        p = self.p
        for e in range(1, p.across):
            self.x_copy(d, e, p.row(p.z_at(-d), p.x_at(-e))).wait_recv()

    def finish(self, over_z, over_x):
        p = self.p
        for d in over_z:
            self.z_copy(d, p.me, self.own).wait_send()
        for d in over_x:
            row = p.row(p.z_at(-d), p.x)
            for e in range(1, p.across):
                self.x_copy(d, e, row).wait_send()


def gather_sems(rows):
    deep, across = lines_of(rows)
    dma = pltpu.SemaphoreType.DMA
    line, cross = (deep - 1,), (deep, across - 1)
    return [dma(line), dma(line), dma(cross), dma(cross)]


def hidden_kernel(
    rows, tile, cot_ref, in_ref, gate_ref, up_ref, down_ref,
    cot_out, in_out, hidden_ref, gg_ref, gu_ref,
    down, held, part, theirs, gates, ups,
    z_send, z_recv, x_send, x_recv, iz_send, iz_recv, ix_send, ix_recv,
    p_send, p_recv, s_send, s_recv, local,
):
    p = Place(rows)
    steps = steps_of(p.deep)
    early = p.deep // 2
    col = lax.axis_index("col")
    deep, half = p.deep, p.deep // 2
    size = p.across * cot_ref.shape[0]
    depth, ff = cot_ref.shape[1], down_ref.shape[0]
    get_own = pltpu.make_async_copy(cot_ref, held.at[p.me], local.at[0])
    get_down = pltpu.make_async_copy(down_ref, down, local.at[1])
    mine = pl.ds(col * half, half)
    get_gate = pltpu.make_async_copy(gate_ref, gates.at[mine], local.at[2])
    get_up = pltpu.make_async_copy(up_ref, ups.at[mine], local.at[3])
    put_own = pltpu.make_async_copy(in_ref, in_out.at[p.me], local.at[4])
    get_own.start()
    get_down.start()
    put_own.start()
    get_gate.start()
    get_up.start()
    p.greet(True)

    def saved(n, src, dst, at):
        return pltpu.make_async_remote_copy(
            src_ref=src, dst_ref=dst.at[pl.ds(at * half, half)],
            send_sem=s_send.at[n], recv_sem=s_recv.at[n],
            device_id={"col": 1 - col}, device_id_type=MESH,
        )

    def share(d):
        return pltpu.make_async_remote_copy(
            src_ref=part.at[d], dst_ref=theirs.at[d],
            send_sem=p_send.at[d], recv_sem=p_recv.at[d],
            device_id={"col": 1 - col}, device_id_type=MESH,
        )

    gather = Gather(p, cot_ref, held, z_send, z_recv, x_send, x_recv)
    ins = Gather(p, in_ref, in_out, iz_send, iz_recv, ix_send, ix_recv)
    gather.along_z(steps[1])
    gather.own_over_x()
    saved(0, gate_ref, gates, col).start()
    saved(1, up_ref, ups, col).start()
    get_own.wait()
    get_down.wait()

    def activations(d):
        z = p.z_at(-d)
        share(d).wait_recv()

        def some(i, carry):
            at = pl.ds(pl.multiple_of(i * 16, 16), 16)
            outs = swiglu_back(gates[z, at, :], ups[z, at, :], part[d, at, :] + theirs[d, at, :])
            for ref, value in zip((hidden_ref, gg_ref, gu_ref), outs):
                ref[z, at, :] = value
            return carry

        lax.fori_loop(0, size // 16, some, 0)

    for k, d in enumerate(steps):
        z = p.z_at(-d)
        if k + 1 < deep:
            gather.arrived(steps[k + 1])
            if k + 2 < deep:
                gather.along_z(steps[k + 2])
            else:
                ins.along_z(steps[1])
            gather.over_x(steps[k + 1])
            if k + 3 == deep:
                ins.own_over_x()
        else:
            for n in range(1, deep - 1):
                ins.arrived(steps[n])
                if n + 1 < deep - 1:
                    ins.along_z(steps[n + 1])
                if n < early:
                    ins.over_x(steps[n])
                if n + 1 == early:
                    break
        gather.group(d)
        left = held[pl.ds(z * p.across, p.across)].reshape(size, depth)

        def some(j, carry):
            at = pl.ds(pl.multiple_of(j * tile, tile), tile)
            part[d, :, at] = lax.dot_general(
                left, down[at, :], COLS, preferred_element_type=jnp.float32
            )
            return carry

        lax.fori_loop(0, ff // tile, some, 0)
        share(d).start()
        if k == 0:
            get_gate.wait()
            get_up.wait()
            saved(0, gate_ref, gates, 1 - col).wait_recv()
            saved(1, up_ref, ups, 1 - col).wait_recv()
        else:
            activations(steps[k - 1])
    put = pltpu.make_async_copy(held, cot_out, local.at[0])
    put.start()
    activations(steps[-1])
    for n in range(early, deep - 1):
        ins.arrived(steps[n])
        if n + 1 < deep - 1:
            ins.along_z(steps[n + 1])
    for d in steps[:early]:
        ins.group(d)
    gather.finish(range(1, deep), range(deep))
    ins.finish(steps[1:-1], steps[:early])
    put_own.wait()
    saved(0, gate_ref, gates, col).wait_send()
    saved(1, up_ref, ups, col).wait_send()
    for d in range(deep):
        share(d).wait_send()
    put.wait()


def inputs_kernel(
    rows, tile, some_ref, gg_ref, gu_ref, gate_ref, up_ref,
    in_out, out_ref,
    gate, up, tot, own, to_x, from_x, to_z, from_z,
    z_send, z_recv, x_send, x_recv, rx_send, rx_recv, rz_send, rz_recv, local,
):
    p = Place(rows)
    deep, across = p.deep, p.across
    steps = steps_of(deep)
    late = steps[deep // 2:]
    tok, depth = out_ref.shape

    def weights(j):
        at = pl.ds(pl.multiple_of(j * tile, tile), tile)
        return [
            pltpu.make_async_copy(ref.at[at, :], to.at[at, :], local.at[n, j])
            for n, (ref, to) in enumerate(((gate_ref, gate), (up_ref, up)))
        ]

    for j in range(depth // tile):
        for copy in weights(j):
            copy.start()
    p.greet(False)
    gather = Gather(p, in_out.at[p.me], in_out, z_send, z_recv, x_send, x_recv)
    for d in late[:-1]:
        gather.over_x(d)
    gather.along_z(late[-1])

    def over_x(d, e):
        return pltpu.make_async_remote_copy(
            src_ref=to_x.at[d, e - 1], dst_ref=from_x.at[d, e - 1],
            send_sem=rx_send.at[d, e - 1], recv_sem=rx_recv.at[d, e - 1],
            device_id={"row": p.row(p.z, p.x_at(e))}, device_id_type=MESH,
        )

    def over_z(d):
        return pltpu.make_async_remote_copy(
            src_ref=to_z.at[d - 1], dst_ref=from_z.at[d - 1],
            send_sem=rz_send.at[d - 1], recv_sem=rz_recv.at[d - 1],
            device_id={"row": p.row(p.z_at(d), p.x)}, device_id_type=MESH,
        )

    def columns(step):
        def some(j, carry):
            step(j, pl.ds(pl.multiple_of(j * tile, tile), tile))
            return carry

        lax.fori_loop(0, depth // tile, some, 0)

    def along_x(d, at):
        total = own[d, :, at]
        for e in range(1, across):
            total += from_x[d, e - 1, :, at].astype(jnp.float32)
        return total

    def pass_on(d):
        for e in range(1, across):
            over_x(d, e).wait_recv()

        def step(j, at):
            to_z[d - 1, :, at] = along_x(d, at).astype(jnp.bfloat16)

        columns(step)
        over_z(d).start()

    order = steps[:0:-1] + [0]
    for n, d in enumerate(order):
        z = p.z_at(d)

        def step(j, at):
            if n == 0:
                for copy in weights(j):
                    copy.wait()
            total = lax.dot_general(
                gg_ref[z], gate[at, :], COLS, preferred_element_type=jnp.float32
            ) + lax.dot_general(gu_ref[z], up[at, :], COLS, preferred_element_type=jnp.float32)
            tot[...] = total.reshape(across, tok, tile)
            own[d, :, at] = tot[p.x]
            for e in range(1, across):
                to_x[d, e - 1, :, at] = tot[p.x_at(e)].astype(jnp.bfloat16)

        columns(step)
        for e in range(1, across):
            over_x(d, e).start()
        if n > 1:
            pass_on(order[n - 2])
    gather.arrived(late[-1])
    gather.over_x(late[-1])
    pass_on(order[deep - 2])
    for e in range(1, across):
        over_x(0, e).wait_recv()
    for d in range(1, deep):
        over_z(d).wait_recv()

    def step(j, at):
        total = along_x(0, at)
        for d in range(1, deep):
            total += from_z[d - 1, :, at].astype(jnp.float32)
        out_ref[:, at] = total.astype(jnp.bfloat16)

    columns(step)
    for d in late:
        gather.group(d)
    gather.finish(late[-1:], late)
    for d in range(deep):
        for e in range(1, across):
            over_x(d, e).wait_send()
    for d in range(1, deep):
        over_z(d).wait_send()


def per_device(inputs, gate_saved, up_saved, cotangent, gate_weight, up_weight, down_weight):
    rows, cols = lax.axis_size("row"), lax.axis_size("col")
    deep, across = lines_of(rows)
    tok, depth = cotangent.shape
    ff = down_weight.shape[0]
    size = tok * across
    if cols != 2 or tok % 16 or deep % 2 or deep < 4 or across < 2 or ff % 256 or depth % 256:
        return plain(
            inputs, gate_saved, up_saved, cotangent, gate_weight, up_weight, down_weight
        )
    bf16, f32 = jnp.bfloat16, jnp.float32
    dma, shape = pltpu.SemaphoreType.DMA, jax.ShapeDtypeStruct
    vmem, anywhere = pl.BlockSpec(memory_space=pltpu.VMEM), pl.BlockSpec(memory_space=pl.ANY)
    tile = 256 if ff % 512 or depth % 512 else 512
    halves = (deep // 2, size, ff)
    cot_all, inputs_some, hidden, gg, gu = pl.pallas_call(
        functools.partial(hidden_kernel, rows, tile),
        in_specs=[anywhere] * 5,
        out_specs=[anywhere, anywhere, vmem, vmem, vmem],
        out_shape=[shape((rows, tok, depth), bf16)] * 2 + [shape((deep, size, ff), bf16)] * 3,
        scratch_shapes=[
            pltpu.VMEM((ff, depth), bf16),
            pltpu.VMEM((rows, tok, depth), bf16),
            pltpu.VMEM((deep, size, ff), f32),
            pltpu.VMEM((deep, size, ff), f32),
            pltpu.VMEM((deep, size, ff), bf16),
            pltpu.VMEM((deep, size, ff), bf16),
            *gather_sems(rows),
            *gather_sems(rows),
            dma((deep,)), dma((deep,)), dma((2,)), dma((2,)), dma((5,)),
        ],
        cost_estimate=pl.CostEstimate(
            flops=2 * rows * tok * depth * ff, bytes_accessed=2 * ff * depth, transcendentals=0
        ),
        compiler_params=pltpu.CompilerParams(
            collective_id=0, has_side_effects=True, vmem_limit_bytes=58 * 2**20
        ),
    )(cotangent, inputs, gate_saved.reshape(halves), up_saved.reshape(halves), down_weight)
    inputs_all, grad_inputs = pl.pallas_call(
        functools.partial(inputs_kernel, rows, tile),
        in_specs=[anywhere, vmem, vmem, anywhere, anywhere],
        out_specs=[anywhere, vmem],
        out_shape=[shape((rows, tok, depth), bf16), shape((tok, depth), bf16)],
        scratch_shapes=[
            pltpu.VMEM((depth, ff), bf16),
            pltpu.VMEM((depth, ff), bf16),
            pltpu.VMEM((across, tok, tile), f32),
            pltpu.VMEM((deep, tok, depth), f32),
            pltpu.VMEM((deep, across - 1, tok, depth), bf16),
            pltpu.VMEM((deep, across - 1, tok, depth), bf16),
            pltpu.VMEM((deep - 1, tok, depth), bf16),
            pltpu.VMEM((deep - 1, tok, depth), bf16),
            *gather_sems(rows),
            *gather_sems(rows)[2:],
            *gather_sems(rows)[:2],
            dma((2, depth // tile)),
        ],
        input_output_aliases={0: 0},
        cost_estimate=pl.CostEstimate(
            flops=4 * rows * tok * depth * ff, bytes_accessed=4 * ff * depth, transcendentals=0
        ),
        compiler_params=pltpu.CompilerParams(
            collective_id=1, has_side_effects=True, vmem_limit_bytes=58 * 2**20
        ),
    )(inputs_some, gg, gu, gate_weight, up_weight)
    flat = lambda a: a.reshape(-1, a.shape[-1])
    (grad_down,) = weight_grads(flat(hidden), (flat(cot_all),), max(1, ff // 256))
    grad_gate, grad_up = weight_grads(flat(inputs_all), (flat(gg), flat(gu)), 8)
    return (grad_inputs, grad_gate, grad_up, grad_down)


def solution(mesh):
    return jax.shard_map(
        per_device,
        mesh=mesh,
        in_specs=(
            P(("groups", "row"), "col"),
            P(("groups", "col"), "row"),
            P(("groups", "col"), "row"),
            P(("groups", "row"), "col"),
            P("col", "row"),
            P("col", "row"),
            P("row", "col"),
        ),
        out_specs=(
            P(("groups", "row"), "col"),
            P(("groups", "col"), "row"),
            P(("groups", "col"), "row"),
            P(("groups", "row"), "col"),
        ),
        check_vma=False,
    )
```
